32 devices in a mesh: groups: 2 (over y), aux: 4 (over z), orb: 2 (over x), rep: 2 (over core).
Axes of the slice: x: 2, y: 2, z: 4, core: 2. Of those that a mesh axis runs over, the one named last changes fastest.
Arguments:
- integrals: bfloat16 [64, 64, 4096], P(('groups', 'aux')), parts along dimension 0, may hold values from -6 to 6
- block_list: int32 [64, 3], P(('groups', 'aux')), parts along dimension 0, may hold values from 0 to 159, as said below
- occupied: bfloat16 [20480, 512], P('groups', ('orb', 'rep')), parts along dimension 0, may hold values from -0.03125 to 0.03125
- owned_blocks: int32 [320], P('groups'), parts along dimension 0, may hold values from 0 to 159
Outputs:
- exchange_slab: float32 [20480, 128], P(('groups', 'aux', 'orb', 'rep')), parts along dimension 0
The draws below stay inside these ranges and needn't reach their ends.
There are 2 independent parts, one for each index of `groups`. The reference program is written for one: setup_inputs(seed, part) draws one part's arguments, and reference() takes and returns one part's arrays. A program takes and returns all parts, laid end to end along the dimension named above; each array names one. Nothing has to cross between parts.
Inputs may be any that keep to these rules, and one draw needn't show every extreme that they name: `block_list`: owned_blocks is a permutation of the 160 orbital blocks. The auxiliary column is below 4. Among the 8 rows of one aux index, at most 4 have a mu block owned by any one aux index; exactly 4 have one owned by aux index 0, and among those each of the first 2 entries of owned_blocks appears.
All inputs are finite; a program needn't handle non-finite values.
Results may differ from the reference program's by a relative error of at most 0.0003.
Values may be sent and summed in bfloat16 or wider, within the bound.
A program may use at most 192 MiB of HBM per device.

```python
import jax
import jax.numpy as jnp
from jax import lax

NBF = 10240
NOCC = 512
BLK = 64
AUXB = 4
SLABB = 2
NBLK = 8
NMUB = 160
MUB_DEV = 40
CAP = 4
SLAB = 128
N_AUX = 4
N_ORB = 2
N_REP = 2


def shared_order(key):
    return jax.random.permutation(key, NMUB).astype(jnp.int32)


def draw_owned_blocks(key, part):
    return shared_order(key)


def one_source(key, order):
    keys = jax.random.split(key, 5)
    labels = jnp.arange(N_AUX * CAP, dtype=jnp.int32) // CAP
    others = jax.random.permutation(keys[0], N_AUX * CAP - CAP).astype(jnp.int32) + CAP
    target = jnp.concatenate([jnp.zeros((CAP,), jnp.int32), labels[others[:NBLK - CAP]]])
    first_rows = jnp.arange(CAP, dtype=jnp.int32) % SLABB
    other_rows = jax.random.randint(keys[1], (NBLK - CAP,), 0, MUB_DEV).astype(jnp.int32)
    local_row = jnp.concatenate([first_rows, other_rows])
    mu_block = order[target * MUB_DEV + local_row]
    aux_block = jax.random.randint(keys[2], (NBLK,), 0, AUXB).astype(jnp.int32)
    nu_block = jax.random.randint(keys[3], (NBLK,), 0, NMUB).astype(jnp.int32)
    table = jnp.stack([aux_block, mu_block, nu_block], axis=1)
    shuffle = jax.random.permutation(keys[4], NBLK)
    return table[shuffle]


def draw_block_list(key, part):
    order = shared_order(key)
    key = jax.random.fold_in(key, 2)
    keys = jax.random.split(key, N_AUX)
    tables = jax.vmap(lambda k: one_source(k, order))(keys)
    return tables.reshape(N_AUX * NBLK, 3).astype(jnp.int32)


def shard_levels(rng, extent, cuts, least, top_value):
    factor_of = 1.0
    for dim, parts in cuts:
        draws = jax.random.uniform(jax.random.fold_in(jax.random.fold_in(rng, 6), dim), (parts,), jnp.float32, least / len(cuts), top_value / len(cuts))
        factor_of = factor_of * jnp.repeat(jnp.exp(draws), extent[dim] // parts).reshape((-1,) + (1,) * (len(extent) - 1 - dim))
    return factor_of


def scatter_about(key, shape, spread, reach, cuts=(), kind=jnp.bfloat16):
    level = shard_levels(key, shape, cuts, -0.22, 0.18) if cuts else 1.0
    entries = jax.random.normal(key, shape, jnp.float32) * spread * level
    return jnp.minimum(jnp.maximum(entries, -reach), reach).astype(kind)


def setup_inputs(seed: int = 0, part: int = 0) -> dict:
    seeds = jax.random.split(jax.random.key(seed), 5)
    part_keys = jax.random.split(jax.random.fold_in(seeds[4], part), 5)
    return {
        "integrals": scatter_about(part_keys[0], (N_AUX * NBLK, BLK, BLK * BLK), 1.0, 6.0, ((0, 4),)),
        "block_list": draw_block_list(jax.random.fold_in(jax.random.fold_in(seeds[4], part), 71), part),
        "occupied": scatter_about(part_keys[2], (NBF, NOCC), (BLK * NOCC) ** -0.5, 0.03125, ((1, 4),)),
        "owned_blocks": draw_owned_blocks(jax.random.fold_in(jax.random.fold_in(seeds[4], part), 71), part),
    }


def reference(integrals, block_list, occupied, owned_blocks):
    width = NOCC // (N_ORB * N_REP)
    cube = integrals.reshape(-1, BLK, BLK, BLK).astype(jnp.float32)
    position = jnp.zeros((NMUB,), jnp.int32).at[owned_blocks].set(jnp.arange(NMUB, dtype=jnp.int32))
    segment = (block_list[:, 0] * NMUB + position[block_list[:, 1]]).astype(jnp.int32)
    coeff = occupied.reshape(NMUB, BLK, NOCC)

    def one_span(total, start):
        cols = lax.dynamic_slice_in_dim(coeff, start, width, 2)
        rows = cols[block_list[:, 2]].astype(jnp.float32)
        pieces = jnp.einsum("kpmn,kni->kpmi", cube, rows).astype(jnp.bfloat16)
        summed = jax.ops.segment_sum(pieces.astype(jnp.float32), segment, num_segments=AUXB * NMUB)
        fields = summed.reshape(AUXB, NMUB, BLK, BLK, width)
        slab = lax.optimization_barrier(fields[:, :SLABB].astype(jnp.bfloat16)).astype(jnp.float32)
        term = jnp.einsum("ajpmi,aspni->jmsn", fields, slab, precision=lax.Precision.HIGHEST)
        return total + term.reshape(NBF, SLAB), None

    starts = jnp.arange(N_ORB * N_REP, dtype=jnp.int32) * width
    total, _ = lax.scan(one_span, jnp.zeros((NBF, SLAB), jnp.float32), starts)
    return total
```

```python
import functools

import jax
import jax.numpy as jnp
from jax import lax
from jax.experimental import pallas as pl
from jax.experimental.pallas import tpu as pltpu
from jax.sharding import PartitionSpec as P

SLABB = 2


def rows_of(block):
    depth, merged = block.shape
    chunks = merged // 128
    stacked = jnp.stack([block[:, c * 128:(c + 1) * 128] for c in range(chunks)], axis=0)
    return jnp.swapaxes(stacked, 0, 1).reshape(depth * chunks, 128)


def put_piece(block, coeff, diag_ref, out_ref, row):
    side, width = coeff.shape
    depth = block.shape[0]
    chunks = side // 2
    diag_ref[0:side, 0:width] = coeff
    diag_ref[side:2 * side, width:2 * width] = coeff
    piece = jnp.dot(rows_of(block), diag_ref[...], preferred_element_type=jnp.float32)
    piece = piece.astype(jnp.bfloat16)
    for p in range(depth):
        for half in range(2):
            out_ref[pl.ds(row + half * chunks, chunks), p * width:(p + 1) * width] = piece[
                p * chunks:(p + 1) * chunks, half * width:(half + 1) * width
            ]


def contract(left_ref, right_ref, total_ref):
    depth = left_ref.shape[1]
    step = min(2048, depth)
    total_ref[...] = jnp.zeros_like(total_ref)

    def body(j, carry):
        cols = pl.ds(pl.multiple_of(j * step, step), step)
        total_ref[...] += lax.dot_general(
            left_ref[:, cols],
            right_ref[:, cols],
            (((1,), (1,)), ((), ())),
            preferred_element_type=jnp.float32,
        )
        return carry

    lax.fori_loop(0, depth // step, body, 0)


def kernel(own_ref, slab_ref, cown_ref, cslab_ref, same_ref, cross_ref, out_ref,
           left, right, total, acc, diag):
    own_count = own_ref.shape[0]
    sources, capacity = slab_ref.shape[0], slab_ref.shape[1]
    side = cown_ref.shape[1]
    diag[...] = jnp.zeros_like(diag)

    def own_body(k, carry):
        put_piece(own_ref[k], cown_ref[k], diag, left, pl.multiple_of(k * side, side))
        return carry

    lax.fori_loop(0, own_count, own_body, 0)
    acc[...] = jnp.zeros_like(acc)

    def source_body(z, carry):
        def slot_body(j, inner):
            put_piece(slab_ref[z, j], cslab_ref[z, j], diag, right, pl.multiple_of(j * side, side))
            return inner

        lax.fori_loop(0, capacity, slot_body, 0)
        contract(left, right, total)
        for pair in range(capacity // 2):
            tile = total[:, pair * 128:(pair + 1) * 128].reshape(own_count, side, 128)
            turned = pltpu.roll(total[:, pair * 128:(pair + 1) * 128], 64, 1)
            turned = turned.reshape(own_count, side, 128)
            index = z * (capacity // 2) + pair
            acc[...] += tile * same_ref[index] + turned * cross_ref[index]
        return carry

    lax.fori_loop(0, sources, source_body, 0)
    out_ref[...] = acc[...]


def local_product(own, slab, cown, cslab, same, cross):
    own_count, depth, merged = own.shape
    sources, capacity = slab.shape[0], slab.shape[1]
    side, width = cown.shape[1], cown.shape[2]
    vmem = pl.BlockSpec(memory_space=pltpu.VMEM)
    return pl.pallas_call(
        kernel,
        out_shape=jax.ShapeDtypeStruct((own_count, side, 2 * side), jnp.float32),
        in_specs=[vmem] * 6,
        out_specs=vmem,
        scratch_shapes=[
            pltpu.VMEM((own_count * side, depth * width), jnp.bfloat16),
            pltpu.VMEM((capacity * side, depth * width), jnp.bfloat16),
            pltpu.VMEM((own_count * side, capacity * side), jnp.float32),
            pltpu.VMEM((own_count, side, 2 * side), jnp.float32),
            pltpu.VMEM((2 * side, 2 * width), jnp.bfloat16),
        ],
        compiler_params=pltpu.CompilerParams(vmem_limit_bytes=48 * 1024 * 1024),
    )(own, slab, cown, cslab, same, cross)


def shards(integrals, block_list, occupied, owned_blocks):
    block_count, aux_functions, merged = integrals.shape
    aux_count = lax.axis_size("aux")
    ranks = lax.axis_size("orb") * lax.axis_size("rep")
    rank = lax.axis_index("orb") * lax.axis_size("rep") + lax.axis_index("rep")
    orbital_blocks = owned_blocks.shape[0]
    owned_count = orbital_blocks // aux_count
    side = occupied.shape[0] // orbital_blocks
    width = occupied.shape[1]
    depth = aux_functions // ranks
    capacity = max(2, (2 * block_count + aux_count - 1) // aux_count)

    matches = owned_blocks[None, :] == block_list[:, 1:2]
    position = jnp.sum(
        jnp.where(matches, jnp.arange(orbital_blocks, dtype=jnp.int32)[None, :], 0), axis=1
    )
    numbers = jnp.arange(block_count, dtype=jnp.int32)
    in_slab = (position < SLABB).astype(jnp.int32)
    ranking = jnp.cumsum(in_slab) - in_slab
    slots = jnp.arange(capacity, dtype=jnp.int32)
    chosen = (ranking[None, :] == slots[:, None]) & (in_slab > 0)[None, :]
    slot_block = jnp.sum(jnp.where(chosen, numbers[None, :], 0), axis=1)
    slot_valid = jnp.any(chosen, axis=1).astype(jnp.int32)
    slot_key = jnp.where(
        slot_valid > 0, block_list[slot_block, 0] * SLABB + position[slot_block], -1
    )
    slot_info = jnp.stack([slot_key, block_list[slot_block, 2]], axis=1)
    all_info = lax.all_gather(slot_info, "aux")

    part = lax.dynamic_slice_in_dim(integrals, rank * depth, depth, axis=1)
    slab = lax.all_gather(part[slot_block], "aux")

    coeff = occupied.reshape(orbital_blocks, side, width)
    needed = jnp.concatenate([block_list[:, 2], all_info[:, :, 1].reshape(-1)])
    rows = lax.all_gather(coeff[needed], ("orb", "rep"), axis=2, tiled=True)
    cown = rows[:block_count]
    cslab = rows[block_count:].reshape(aux_count, capacity, side, width * ranks)

    keys = all_info[:, :, 0].reshape(-1, 2)
    hit = (
        keys[:, None, :, None]
        == (block_list[:, 0:1] * SLABB + jnp.arange(SLABB, dtype=jnp.int32)[None, :])[None, :, None, :]
    ).astype(jnp.float32)
    same = jnp.stack([hit[:, :, 0, 0], hit[:, :, 1, 1]], axis=2)
    cross = jnp.stack([hit[:, :, 1, 0], hit[:, :, 0, 1]], axis=2)
    same = jnp.repeat(same, side, axis=2)[:, :, None, :]
    cross = jnp.repeat(cross, side, axis=2)[:, :, None, :]
    blocks = local_product(part, slab, cown, cslab, same, cross)
    half = side // 2
    blocks = blocks.reshape(block_count, 2, half, SLABB, 2, half)
    blocks = blocks.transpose(0, 2, 1, 3, 5, 4).reshape(block_count, side, SLABB * side)

    summed = lax.psum_scatter(blocks, ("orb", "rep"), scatter_dimension=1, tiled=True)
    everything = lax.all_gather(summed, ("aux", "orb", "rep"))
    everything = everything.reshape(aux_count, ranks, block_count, side // ranks, SLABB * side)
    everything = everything.transpose(0, 2, 1, 3, 4).reshape(aux_count * block_count, -1)
    all_positions = lax.all_gather(position, "aux").reshape(-1)
    base = lax.axis_index("aux") * owned_count
    mine = owned_count // ranks
    if owned_count % ranks:
        mine = owned_count
    else:
        base = base + rank * mine
    grouping = (
        all_positions[None, :] == (base + jnp.arange(mine, dtype=jnp.int32))[:, None]
    ).astype(jnp.float32)
    out = jnp.dot(grouping, everything, precision=lax.Precision.HIGHEST)
    out = out.reshape(mine * side, SLABB * side)
    kept = owned_count * side // ranks
    if mine * side != kept:
        out = lax.dynamic_slice_in_dim(out, rank * kept, kept, axis=0)
    return out


def solution(mesh):
    in_specs = (
        P(("groups", "aux"), None, None),
        P(("groups", "aux"), None),
        P("groups", ("orb", "rep")),
        P("groups"),
    )
    out_specs = P(("groups", "aux", "orb", "rep"), None)
    return jax.shard_map(shards, mesh=mesh, in_specs=in_specs, out_specs=out_specs, check_vma=False)
```

```python
import functools

import jax
import jax.numpy as jnp
from jax import lax
from jax.experimental import pallas as pl
from jax.experimental.pallas import tpu as pltpu
from jax.sharding import PartitionSpec as P

SLABB = 2
MESH = pl.DeviceIdType.MESH


def rows_of(block):
    depth, merged = block.shape
    chunks = merged // 128
    stacked = jnp.stack([block[:, c * 128:(c + 1) * 128] for c in range(chunks)], axis=0)
    return jnp.swapaxes(stacked, 0, 1).reshape(depth * chunks, 128)


def put_piece(block, coeff, diag_ref, out_ref, row):
    ranks = len(coeff)
    side, width = coeff[0].shape
    full = ranks * width
    depth = block.shape[0]
    chunks = side // 2
    for r in range(ranks):
        diag_ref[0:side, r * width:(r + 1) * width] = coeff[r]
        diag_ref[side:2 * side, full + r * width:full + (r + 1) * width] = coeff[r]
    piece = jnp.dot(rows_of(block), diag_ref[...], preferred_element_type=jnp.float32)
    piece = piece.astype(jnp.bfloat16)
    for p in range(depth):
        for half in range(2):
            out_ref[pl.ds(row + half * chunks, chunks), p * full:(p + 1) * full] = piece[
                p * chunks:(p + 1) * chunks, half * full:(half + 1) * full
            ]


def contract(left_ref, right_ref, total_ref):
    depth = left_ref.shape[1]
    step = min(2048, depth)
    total_ref[...] = jnp.zeros_like(total_ref)

    def body(j, carry):
        cols = pl.ds(pl.multiple_of(j * step, step), step)
        total_ref[...] += lax.dot_general(
            left_ref[:, cols],
            right_ref[:, cols],
            (((1,), (1,)), ((), ())),
            preferred_element_type=jnp.float32,
        )
        return carry

    lax.fori_loop(0, depth // step, body, 0)


def kernel(nz, norb, nrep, capacity,
           own_ref, occ_ref, tags_ref, code_ref, lane_ref, nums_ref, place_ref, out_ref,
           slots, buf, tagbuf, tagnum, crows_own, crows, left, right, total, acc, diag,
           natural, reduced, outgoing, incoming, grouped,
           up_sem, down_sem, recv_sem, tag_send, tag_recv, num_sem,
           own_send, own_recv, row_send, row_recv,
           a_send, a_recv, b_send, b_recv, c_send, c_recv):
    z = lax.axis_index("aux")
    rank = lax.axis_index("orb") * nrep + lax.axis_index("rep")
    ranks = norb * nrep
    own_count = own_ref.shape[0]
    side = crows_own.shape[2]
    pairs = capacity // 2
    quarter = side // ranks

    def at_z(o):
        return {"aux": lax.rem(z + o, nz)}

    def at_rank(o):
        peer = lax.rem(rank + o, ranks)
        return {"orb": peer // nrep, "rep": lax.rem(peer, nrep)}

    barrier = pltpu.get_barrier_semaphore()
    for o in range(1, nz):
        pl.semaphore_signal(barrier, inc=1, device_id=at_z(o), device_id_type=MESH)
    for o in range(1, ranks):
        pl.semaphore_signal(barrier, inc=1, device_id=at_rank(o), device_id_type=MESH)

    def occupied_rows(block):
        return occ_ref[block]

    for j in range(capacity):
        slots[j] = own_ref[nums_ref[0, j]]
    for k in range(own_count):
        crows_own[rank, k] = occupied_rows(nums_ref[1, k])
    for j in range(capacity):
        crows[rank, z, j] = occupied_rows(nums_ref[2, j])
    diag[...] = jnp.zeros_like(diag)
    acc[...] = jnp.zeros_like(acc)
    pl.semaphore_wait(barrier, nz - 1 + ranks - 1)

    def remote(src, dst, send, recv, where):
        return pltpu.make_async_remote_copy(
            src_ref=src, dst_ref=dst, send_sem=send, recv_sem=recv,
            device_id=where, device_id_type=MESH,
        )

    def tag_copy(o):
        return remote(tags_ref, tagbuf.at[z], tag_send.at[o], tag_recv.at[o], at_z(o))

    def first_up(j):
        return remote(slots.at[j], buf.at[z, j], up_sem.at[z, j], recv_sem.at[z, j], {"aux": z + 1})

    def first_down(j):
        return remote(slots.at[j], buf.at[z, j], down_sem.at[z, j], recv_sem.at[z, j], {"aux": z - 1})

    def pass_up(s, j):
        return remote(buf.at[s, j], buf.at[s, j], up_sem.at[s, j], recv_sem.at[s, j], {"aux": z + 1})

    def pass_down(s, j):
        return remote(buf.at[s, j], buf.at[s, j], down_sem.at[s, j], recv_sem.at[s, j], {"aux": z - 1})

    def own_copy(o):
        return remote(crows_own.at[rank], crows_own.at[rank], own_send.at[o], own_recv.at[o], at_rank(o))

    def row_copy(o, s):
        return remote(crows.at[rank, s], crows.at[rank, s], row_send.at[o, s], row_recv.at[o, s], at_rank(o))

    has_up = z < nz - 1
    has_down = z > 0
    for o in range(1, nz):
        tag_copy(o).start()
    for o in range(1, ranks):
        own_copy(o).start()
    for j in range(capacity):
        @pl.when(has_up)
        def _():
            first_up(j).start()

        @pl.when(has_down)
        def _():
            first_down(j).start()
    for o in range(1, ranks):
        row_copy(o, z).start()

    for o in range(1, nz):
        s = lax.rem(z + nz - o, nz)
        tag_copy(o).wait_recv()
        number_copy = pltpu.make_async_copy(tagbuf.at[s], tagnum.at[s], num_sem.at[o])
        number_copy.start()
        number_copy.wait()
        for j in range(capacity):
            crows[rank, s, j] = occupied_rows(tagnum[s, 2 * pairs, j])
        for p in range(1, ranks):
            row_copy(p, s).start()

    for o in range(1, ranks):
        own_copy(o).wait_recv()

    def own_body(k, carry):
        coeff = [crows_own[r, k] for r in range(ranks)]
        put_piece(own_ref[k], coeff, diag, left, pl.multiple_of(k * side, side))
        return carry

    lax.fori_loop(0, own_count, own_body, 0)

    def add_source(same_of):
        contract(left, right, total)
        for pair in range(pairs):
            tile = total[:, pair * 128:(pair + 1) * 128]
            turned = pltpu.roll(tile, 64, 1).reshape(own_count, side, 128)
            tile = tile.reshape(own_count, side, 128)
            same = (same_of(pair)[None] == code_ref[...])
            cross = (same_of(pairs + pair)[None] == code_ref[...])
            acc[...] += jnp.where(same, tile, 0.0) + jnp.where(cross, turned, 0.0)

    def piece_of(block, s, j):
        coeff = [crows[r, s, j] for r in range(ranks)]
        put_piece(block, coeff, diag, right, pl.multiple_of(j * side, side))

    for o in range(1, ranks):
        row_copy(o, z).wait_recv()

    def own_slot(j, carry):
        piece_of(slots[j], z, j)
        return carry

    lax.fori_loop(0, capacity, own_slot, 0)
    add_source(lambda row: tags_ref[row:row + 1, :])

    def distance_body(d, carry):
        low = z - d
        high = z + d

        def arrive(j, inner):
            @pl.when(low >= 0)
            def _():
                pass_up(low, j).wait_recv()

                @pl.when(has_up)
                def _():
                    pass_up(low, j).start()

            @pl.when(high < nz)
            def _():
                pass_down(high, j).wait_recv()

                @pl.when(has_down)
                def _():
                    pass_down(high, j).start()

            return inner

        lax.fori_loop(0, capacity, arrive, 0)

        def side_body(which, inner):
            s = z + (2 * which - 1) * d

            @pl.when((s >= 0) & (s < nz))
            def _():
                for o in range(1, ranks):
                    row_copy(o, s).wait_recv()

                def slot_body(j, deep):
                    piece_of(buf[s, j], s, j)
                    return deep

                lax.fori_loop(0, capacity, slot_body, 0)
                add_source(lambda row: tagbuf[s, row:row + 1, :])

            return inner

        lax.fori_loop(0, 2, side_body, 0)
        return carry

    lax.fori_loop(1, nz, distance_body, 0)

    half = side // 2
    flat = jnp.dot(
        acc[...].reshape(own_count * side, 2 * side), lane_ref[...],
        precision=lax.Precision.HIGHEST, preferred_element_type=jnp.float32,
    )
    for k in range(own_count):
        for part in range(2):
            start = k * side + part * half
            natural[k, pl.ds(part, half, stride=2), :] = flat[start:start + half]

    def a_copy(o):
        peer = lax.rem(rank + o, ranks)
        return remote(
            natural.at[:, pl.ds(pl.multiple_of(peer * quarter, quarter), quarter), :],
            reduced.at[rank], a_send.at[o], a_recv.at[o], at_rank(o),
        )

    for o in range(1, ranks):
        a_copy(o).start()
    reduced[rank] = natural[:, pl.ds(pl.multiple_of(rank * quarter, quarter), quarter), :]
    for o in range(1, ranks):
        a_copy(o).wait_recv()
    summed = reduced[0]
    for r in range(1, ranks):
        summed = summed + reduced[r]

    for t in range(nz):
        for c in range(capacity):
            picked = summed[0] * place_ref[t * capacity + c, 0]
            for k in range(1, own_count):
                picked = picked + summed[k] * place_ref[t * capacity + c, k]
            outgoing[t, c] = picked

    def b_copy(o):
        peer = lax.rem(z + o, nz)
        return remote(outgoing.at[peer], incoming.at[z], b_send.at[o], b_recv.at[o], at_z(o))

    for o in range(1, nz):
        b_copy(o).start()
    incoming[z] = outgoing[z]
    for c in range(capacity):
        tagnum[z, 2 * pairs + 1, z * capacity + c] = nums_ref[3, z * capacity + c]
    for o in range(1, nz):
        b_copy(o).wait_recv()

    def group_body(row, carry):
        value = jnp.zeros((quarter, 2 * side), jnp.float32)
        for s in range(nz):
            for c in range(capacity):
                tag = jnp.full(value.shape, tagnum[s, 2 * pairs + 1, z * capacity + c], jnp.int32)
                value = value + jnp.where(tag == row, incoming[s, c], 0.0)
        grouped[row] = value
        return carry

    lax.fori_loop(0, grouped.shape[0], group_body, 0)

    mine = out_ref.shape[0]
    split = mine != grouped.shape[0]

    def c_copy(o):
        peer = lax.rem(rank + o, ranks)
        base = peer * mine if split else 0
        return remote(
            grouped.at[pl.ds(base, mine)],
            out_ref.at[:, pl.ds(pl.multiple_of(rank * quarter, quarter), quarter), :],
            c_send.at[o], c_recv.at[o], at_rank(o),
        )

    for o in range(1, ranks):
        c_copy(o).start()
    base = rank * mine if split else 0
    out_ref[:, pl.ds(pl.multiple_of(rank * quarter, quarter), quarter), :] = grouped[
        pl.ds(base, mine)
    ]
    for o in range(1, ranks):
        c_copy(o).wait_recv()

    for o in range(1, nz):
        tag_copy(o).wait_send()
        b_copy(o).wait_send()
    for o in range(1, ranks):
        own_copy(o).wait_send()
        a_copy(o).wait_send()
        c_copy(o).wait_send()

    def sent_rows(s, carry):
        for o in range(1, ranks):
            row_copy(o, s).wait_send()
        for j in range(capacity):
            @pl.when(has_up & (s <= z))
            def _():
                pass_up(s, j).wait_send()

            @pl.when(has_down & (s >= z))
            def _():
                pass_down(s, j).wait_send()
        return carry

    lax.fori_loop(0, nz, sent_rows, 0)


def exchange(mesh_shape, capacity, mine, owned_count, own, occupied, tags, code, lane, nums, place):
    nz, norb, nrep = mesh_shape
    ranks = norb * nrep
    own_count, depth, merged = own.shape
    width = occupied.shape[2]
    side = lane.shape[0] // SLABB
    full = ranks * width
    quarter = side // ranks
    vmem = pl.BlockSpec(memory_space=pltpu.VMEM)
    smem = pl.BlockSpec(memory_space=pltpu.SMEM)
    dma = pltpu.SemaphoreType.DMA
    return pl.pallas_call(
        functools.partial(kernel, nz, norb, nrep, capacity),
        out_shape=jax.ShapeDtypeStruct((mine, side, SLABB * side), jnp.float32),
        in_specs=[vmem] * 5 + [smem] * 2,
        out_specs=vmem,
        scratch_shapes=[
            pltpu.VMEM((capacity, depth, merged), jnp.bfloat16),
            pltpu.VMEM((nz, capacity, depth, merged), jnp.bfloat16),
            pltpu.VMEM((nz,) + tags.shape, jnp.int32),
            pltpu.SMEM((nz,) + tags.shape, jnp.int32),
            pltpu.VMEM((ranks, own_count, side, width), jnp.bfloat16),
            pltpu.VMEM((ranks, nz, capacity, side, width), jnp.bfloat16),
            pltpu.VMEM((own_count * side, depth * full), jnp.bfloat16),
            pltpu.VMEM((capacity * side, depth * full), jnp.bfloat16),
            pltpu.VMEM((own_count * side, capacity * side), jnp.float32),
            pltpu.VMEM((own_count, side, SLABB * side), jnp.float32),
            pltpu.VMEM((2 * side, 2 * full), jnp.bfloat16),
            pltpu.VMEM((own_count, side, SLABB * side), jnp.float32),
            pltpu.VMEM((ranks, own_count, quarter, SLABB * side), jnp.float32),
            pltpu.VMEM((nz, capacity, quarter, SLABB * side), jnp.float32),
            pltpu.VMEM((nz, capacity, quarter, SLABB * side), jnp.float32),
            pltpu.VMEM((owned_count, quarter, SLABB * side), jnp.float32),
            dma((nz, capacity)), dma((nz, capacity)), dma((nz, capacity)),
            dma((nz,)), dma((nz,)), dma((nz,)),
            dma((ranks,)), dma((ranks,)), dma((ranks, nz)), dma((ranks, nz)),
            dma((ranks,)), dma((ranks,)), dma((nz,)), dma((nz,)), dma((ranks,)), dma((ranks,)),
        ],
        compiler_params=pltpu.CompilerParams(
            vmem_limit_bytes=48 * 1024 * 1024, collective_id=0, has_side_effects=True
        ),
    )(own, occupied, tags, code, lane, nums, place)


def shards(integrals, block_list, occupied, owned_blocks):
    block_count, aux_functions, merged = integrals.shape
    aux_count = lax.axis_size("aux")
    norb, nrep = lax.axis_size("orb"), lax.axis_size("rep")
    ranks = norb * nrep
    rank = lax.axis_index("orb") * nrep + lax.axis_index("rep")
    orbital_blocks = owned_blocks.shape[0]
    owned_count = orbital_blocks // aux_count
    side = occupied.shape[0] // orbital_blocks
    depth = aux_functions // ranks
    capacity = max(2, (2 * block_count + aux_count - 1) // aux_count)
    pairs = capacity // 2
    slot_count = aux_count * capacity

    matches = owned_blocks[None, :] == block_list[:, 1:2]
    position = jnp.sum(
        jnp.where(matches, jnp.arange(orbital_blocks, dtype=jnp.int32)[None, :], 0), axis=1
    )
    target = position // owned_count
    numbers = jnp.arange(block_count, dtype=jnp.int32)
    before = (target[None, :] == target[:, None]) & (numbers[None, :] < numbers[:, None])
    slot_of = target * capacity + jnp.sum(before.astype(jnp.int32), axis=1)
    chosen = (
        slot_of[None, :] == jnp.arange(slot_count, dtype=jnp.int32)[:, None]
    ).astype(jnp.int32)

    def by_slot(value, empty):
        return jnp.sum(chosen * (value - empty)[None, :], axis=1) + empty

    local_rows = by_slot(position % owned_count, -1)
    slot_block = by_slot(numbers, 0)[:capacity]
    slot_nu = by_slot(block_list[:, 2], 0)[:capacity]
    key = jnp.where(position < SLABB, block_list[:, 0] * SLABB + position, -8)
    slot_key = by_slot(key, -8)[:capacity].reshape(pairs, 2)
    even, odd = slot_key[:, :1], slot_key[:, 1:]
    first = jnp.arange(SLABB * side, dtype=jnp.int32)[None, :] < side
    same = jnp.where(first, even, odd - 1)
    cross = jnp.where(first, odd, even - 1)

    def row(value):
        return jnp.pad(value, (0, SLABB * side - value.shape[0]))[None, :]

    tags = jnp.concatenate([same, cross, row(slot_nu), row(local_rows)], axis=0)
    tags = jnp.pad(tags, ((0, -tags.shape[0] % 8), (0, 0)))
    code = jnp.broadcast_to(
        (block_list[:, 0] * SLABB)[:, None, None], (block_count, 1, SLABB * side)
    )
    nums = jnp.concatenate(
        [row(slot_block), row(block_list[:, 2]), row(slot_nu), row(local_rows)], axis=0
    )
    place = chosen.astype(jnp.float32)
    lanes = jnp.arange(SLABB * side, dtype=jnp.int32)
    inner = lanes % side
    goes = lanes - inner + 2 * (inner % (side // 2)) + inner // (side // 2)
    lane = (goes[:, None] == lanes[None, :]).astype(jnp.float32)

    part = lax.dynamic_slice_in_dim(integrals, rank * depth, depth, axis=1)
    mine = owned_count if owned_count % ranks else owned_count // ranks
    out = exchange(
        (aux_count, norb, nrep), capacity, mine, owned_count,
        part, occupied.reshape(orbital_blocks, side, -1), tags, code, lane, nums, place,
    )
    out = out.reshape(mine * side, SLABB * side)
    kept = owned_count * side // ranks
    if mine * side != kept:
        out = lax.dynamic_slice_in_dim(out, rank * kept, kept, axis=0)
    return out


def solution(mesh):
    in_specs = (
        P(("groups", "aux"), None, None),
        P(("groups", "aux"), None),
        P("groups", ("orb", "rep")),
        P("groups"),
    )
    out_specs = P(("groups", "aux", "orb", "rep"), None)
    return jax.shard_map(shards, mesh=mesh, in_specs=in_specs, out_specs=out_specs, check_vma=False)
```

```python
import functools

import jax
import jax.numpy as jnp
from jax import lax
from jax.experimental import pallas as pl
from jax.experimental.pallas import tpu as pltpu
from jax.sharding import PartitionSpec as P

SLABB = 2
MESH = pl.DeviceIdType.MESH


def rows_of(block):
    depth, merged = block.shape
    chunks = merged // 128
    stacked = jnp.stack([block[:, c * 128:(c + 1) * 128] for c in range(chunks)], axis=0)
    return jnp.swapaxes(stacked, 0, 1).reshape(depth * chunks, 128)


def put_piece(block, coeff, diag_ref, out_ref, row):
    ranks = len(coeff)
    side, width = coeff[0].shape
    full = ranks * width
    chunks = block.shape[1] // 128
    folds = side // 2 // chunks
    depth = block.shape[0] // folds
    for r in range(ranks):
        diag_ref[0:side, r * width:(r + 1) * width] = coeff[r]
        diag_ref[side:2 * side, full + r * width:full + (r + 1) * width] = coeff[r]
    piece = jnp.dot(rows_of(block), diag_ref[...], preferred_element_type=jnp.float32)
    for p in range(depth):
        starts = [(h * depth + p) * chunks for h in range(folds)]
        for half in range(2):
            cols = slice(half * full, (half + 1) * full)
            lines = jnp.concatenate([piece[start:start + chunks, cols] for start in starts], axis=0)
            out_ref[
                row, half * (side // 2):(half + 1) * (side // 2), p * full:(p + 1) * full
            ] = lines.astype(jnp.bfloat16)


def contract(left_ref, right_ref, total_ref):
    depth = left_ref.shape[2]
    step = min(2048, depth)
    total_ref[...] = jnp.zeros_like(total_ref)

    def body(j, carry):
        cols = pl.ds(pl.multiple_of(j * step, step), step)
        total_ref[...] += lax.dot_general(
            left_ref[:, :, cols].reshape(-1, step),
            right_ref[:, :, cols].reshape(-1, step),
            (((1,), (1,)), ((), ())),
            preferred_element_type=jnp.float32,
        )
        return carry

    lax.fori_loop(0, depth // step, body, 0)


def kernel(nz, norb, nrep, capacity,
           own_ref, occ_ref, tags_ref, lane_ref, nums_ref, out_ref,
           slots, pairbuf, buf, tagbuf, tagnum, crows, left, right, total, acc, diag,
           natural, chunked, reduced, outgoing, incoming, grouped,
           pair_send, pair_recv, cross_send, cross_recv, tag_send, tag_recv, num_sem,
           row_send, row_recv, a_send, a_recv, b_send, b_recv, c_send, c_recv):
    z = lax.axis_index("aux")
    low = lax.rem(z, 2)
    mate = z + 1 - 2 * low
    rank = lax.axis_index("orb") * nrep + lax.axis_index("rep")
    ranks = norb * nrep
    count = own_ref.shape[0]
    side = lane_ref.shape[0] // SLABB
    pairs = capacity // 2
    eighth = side // (2 * ranks)
    quarter = 2 * eighth
    row_same, row_nu, row_slot = count, count + 2 * pairs, count + 2 * pairs + 1
    row_local, row_pick = count + 2 * pairs + 2, count + 2 * pairs + 3

    def at_z(o):
        return {"aux": lax.rem(z + o, nz)}

    def at_rank(o):
        peer = lax.rem(rank + o, ranks)
        return {"orb": peer // nrep, "rep": lax.rem(peer, nrep)}

    def at_mate(o):
        peer = lax.rem(rank + o, ranks)
        return {"aux": mate, "orb": peer // nrep, "rep": lax.rem(peer, nrep)}

    barrier = pltpu.get_barrier_semaphore()
    for o in range(1, nz):
        pl.semaphore_signal(barrier, inc=1, device_id=at_z(o), device_id_type=MESH)
    for o in range(1, ranks):
        pl.semaphore_signal(barrier, inc=1, device_id=at_rank(o), device_id_type=MESH)
        pl.semaphore_signal(barrier, inc=1, device_id=at_mate(o), device_id_type=MESH)

    for j in range(capacity):
        slots[j] = own_ref[nums_ref[0, j]]
    for k in range(count):
        crows[rank, z, k] = occ_ref[nums_ref[1, k]]
    pl.semaphore_wait(barrier, nz - 1 + 2 * (ranks - 1))

    def remote(src, dst, send, recv, where):
        return pltpu.make_async_remote_copy(
            src_ref=src, dst_ref=dst, send_sem=send, recv_sem=recv,
            device_id=where, device_id_type=MESH,
        )

    def tag_copy(o):
        return remote(tags_ref, tagbuf.at[z], tag_send.at[o], tag_recv.at[o], at_z(o))

    def pair_copy(k):
        return remote(own_ref.at[k, 1 - low], pairbuf.at[k], pair_send.at[k], pair_recv.at[k], {"aux": mate})

    def cross_copy(o, j):
        peer = lax.rem(z + o, nz)
        return remote(
            slots.at[j, lax.rem(peer, 2)], buf.at[z, j], cross_send.at[o, j], cross_recv.at[o, j], at_z(o)
        )

    def row_copy(o, s, size):
        return remote(
            crows.at[rank, s, pl.ds(0, size)], crows.at[rank, s, pl.ds(0, size)],
            row_send.at[o, s], row_recv.at[o, s], at_rank(o),
        )

    for o in range(1, nz):
        tag_copy(o).start()
    for o in range(1, ranks):
        row_copy(o, z, count).start()
    for k in range(count):
        pair_copy(k).start()
    for j in range(capacity):
        for o in range(1, nz):
            @pl.when(lax.rem(z + o, nz) != mate)
            def _():
                cross_copy(o, j).start()
    diag[...] = jnp.zeros_like(diag)
    acc[...] = jnp.zeros_like(acc)

    for o in range(1, nz):
        s = lax.rem(z + nz - o, nz)
        tag_copy(o).wait_recv()
        number_copy = pltpu.make_async_copy(tagbuf.at[s], tagnum.at[s], num_sem.at[o])
        number_copy.start()
        number_copy.wait()

        @pl.when(s == mate)
        def _():
            for k in range(count):
                crows[rank, s, k] = occ_ref[tagnum[s, row_nu, k]]
            for p in range(1, ranks):
                row_copy(p, s, count).start()

        @pl.when(s != mate)
        def _():
            for j in range(capacity):
                crows[rank, s, j] = occ_ref[tagnum[s, row_slot, j]]
            for p in range(1, ranks):
                row_copy(p, s, capacity).start()

    def half_transform(block, s, j, out_ref, row):
        coeff = [crows[r, s, j] for r in range(ranks)]
        put_piece(block, coeff, diag, out_ref, row)

    for o in range(1, ranks):
        row_copy(o, z, count).wait_recv()

    def own_body(k, carry):
        half_transform(own_ref[k, low], z, k, left, low * count + k)
        return carry

    lax.fori_loop(0, count, own_body, 0)
    for o in range(1, ranks):
        row_copy(o, mate, count).wait_recv()

    def mate_body(k, carry):
        pair_copy(k).wait_recv()
        half_transform(pairbuf[k], mate, k, left, (1 - low) * count + k)
        return carry

    lax.fori_loop(0, count, mate_body, 0)
    for k in range(count):
        tagbuf[z, k:k + 1, :] = tags_ref[k:k + 1, :]

    def add_source(same_of):
        contract(left, right, total)
        for pair in range(pairs):
            for part in range(2):
                tile = total[part * count * side:(part + 1) * count * side, pair * 128:(pair + 1) * 128]
                turned = pltpu.roll(tile, 64, 1).reshape(count, side, 128)
                tile = tile.reshape(count, side, 128)
                code = tagbuf[z - low + part, 0:count, :].reshape(count, 1, 128)
                same = same_of(pair)[None] == code
                cross = same_of(pairs + pair)[None] == code
                acc[part * count:(part + 1) * count] += (
                    jnp.where(same, tile, 0.0) + jnp.where(cross, turned, 0.0)
                )

    for j in range(capacity):
        right[j] = left[nums_ref[0, j] + low * count]
    add_source(lambda row: tags_ref[row_same + row:row_same + row + 1, :])
    for j in range(capacity):
        right[j] = left[tagnum[mate, row_pick, j] + (1 - low) * count]
    add_source(lambda row: tagbuf[mate, row_same + row:row_same + row + 1, :])

    def cross_body(o, carry):
        s = lax.rem(z + nz - o, nz)

        @pl.when(s != mate)
        def _():
            for p in range(1, ranks):
                row_copy(p, s, capacity).wait_recv()

            def slot_body(j, deep):
                cross_copy(o, j).wait_recv()
                half_transform(buf[s, j], s, j, right, j)
                return deep

            lax.fori_loop(0, capacity, slot_body, 0)
            add_source(lambda row: tagbuf[s, row_same + row:row_same + row + 1, :])

        return carry

    lax.fori_loop(1, nz, cross_body, 0)

    half = side // 2
    flat = jnp.dot(
        acc[...].reshape(2 * count * side, 2 * side), lane_ref[...],
        precision=lax.Precision.HIGHEST, preferred_element_type=jnp.float32,
    )
    for k in range(2 * count):
        for part in range(2):
            start = k * side + part * half
            natural[k, pl.ds(part, half, stride=2), :] = flat[start:start + half]
    for k in range(2 * count):
        for m in range(2 * ranks):
            chunked[m, k] = natural[k, m * eighth:(m + 1) * eighth, :]

    spot = 2 * rank + low

    def a_near(o):
        peer = 2 * lax.rem(rank + o, ranks) + low
        return remote(chunked.at[peer], reduced.at[spot], a_send.at[0, o], a_recv.at[0, o], at_rank(o))

    def a_far(o):
        peer = 2 * lax.rem(rank + o, ranks) + 1 - low
        return remote(chunked.at[peer], reduced.at[spot], a_send.at[1, o], a_recv.at[1, o], at_mate(o))

    for o in range(ranks):
        a_far(o).start()
    for o in range(1, ranks):
        a_near(o).start()
    reduced[spot] = chunked[spot]
    for o in range(1, ranks):
        a_near(o).wait_recv()
    for o in range(ranks):
        a_far(o).wait_recv()
    summed = reduced[0]
    for r in range(1, 2 * ranks):
        summed = summed + reduced[r]

    for slot in range(nz * capacity):
        tagnum[z, row_pick, slot] = nums_ref[0, slot]
        tagnum[z, row_local, slot] = nums_ref[2, slot]
    for t in range(nz):
        for part in range(2):
            for c in range(capacity):
                tag = jnp.full(summed.shape[1:], tagnum[z - low + part, row_pick, t * capacity + c], jnp.int32)
                picked = jnp.zeros(summed.shape[1:], jnp.float32)
                for k in range(count):
                    picked = picked + jnp.where(tag == k, summed[part * count + k], 0.0)
                outgoing[t, part * capacity + c] = picked

    def b_copy(o):
        peer = lax.rem(z + o, nz)
        return remote(outgoing.at[peer], incoming.at[z], b_send.at[o], b_recv.at[o], at_z(o))

    for o in range(1, nz):
        b_copy(o).start()
    incoming[z] = outgoing[z]
    for o in range(1, nz):
        b_copy(o).wait_recv()

    def group_body(row, carry):
        for part in range(2):
            value = jnp.zeros((eighth, 2 * side), jnp.float32)
            for s in range(part, nz, 2):
                for c in range(capacity):
                    for shift, source in ((0, s - part), (capacity, s - part + 1)):
                        tag = jnp.full(value.shape, tagnum[source, row_local, z * capacity + c], jnp.int32)
                        value = value + jnp.where(tag == row, incoming[s, shift + c], 0.0)
            grouped[row, part * eighth:(part + 1) * eighth, :] = value
        return carry

    lax.fori_loop(0, grouped.shape[0], group_body, 0)

    mine = out_ref.shape[0]
    split = mine != grouped.shape[0]

    def c_copy(o):
        peer = lax.rem(rank + o, ranks)
        base = peer * mine if split else 0
        return remote(
            grouped.at[pl.ds(base, mine)],
            out_ref.at[:, pl.ds(pl.multiple_of(rank * quarter, quarter), quarter), :],
            c_send.at[o], c_recv.at[o], at_rank(o),
        )

    for o in range(1, ranks):
        c_copy(o).start()
    base = rank * mine if split else 0
    out_ref[:, pl.ds(pl.multiple_of(rank * quarter, quarter), quarter), :] = grouped[
        pl.ds(base, mine)
    ]
    for o in range(1, ranks):
        c_copy(o).wait_recv()

    for k in range(count):
        pair_copy(k).wait_send()
    for o in range(1, nz):
        tag_copy(o).wait_send()
        b_copy(o).wait_send()

        @pl.when(lax.rem(z + o, nz) != mate)
        def _():
            for j in range(capacity):
                cross_copy(o, j).wait_send()
    for o in range(ranks):
        a_far(o).wait_send()
    for o in range(1, ranks):
        a_near(o).wait_send()
        c_copy(o).wait_send()

    def sent_rows(s, carry):
        @pl.when((s == z) | (s == mate))
        def _():
            for o in range(1, ranks):
                row_copy(o, s, count).wait_send()

        @pl.when((s != z) & (s != mate))
        def _():
            for o in range(1, ranks):
                row_copy(o, s, capacity).wait_send()

        return carry

    lax.fori_loop(0, nz, sent_rows, 0)


def exchange(mesh_shape, capacity, mine, owned_count, own, occupied, tags, lane, nums):
    nz, norb, nrep = mesh_shape
    ranks = norb * nrep
    count, _, lines, merged = own.shape
    width = occupied.shape[2]
    side = lane.shape[0] // SLABB
    full = ranks * width
    inner = lines * merged // (side * side) * full
    eighth = side // (2 * ranks)
    vmem = pl.BlockSpec(memory_space=pltpu.VMEM)
    smem = pl.BlockSpec(memory_space=pltpu.SMEM)
    dma = pltpu.SemaphoreType.DMA

    def result(*lead):
        return pltpu.VMEM(lead + (SLABB * side,), jnp.float32)

    return pl.pallas_call(
        functools.partial(kernel, nz, norb, nrep, capacity),
        out_shape=jax.ShapeDtypeStruct((mine, side, SLABB * side), jnp.float32),
        in_specs=[vmem] * 4 + [smem],
        out_specs=vmem,
        scratch_shapes=[
            pltpu.VMEM((capacity, 2, lines, merged), jnp.bfloat16),
            pltpu.VMEM((count, lines, merged), jnp.bfloat16),
            pltpu.VMEM((nz, capacity, lines, merged), jnp.bfloat16),
            pltpu.VMEM((nz,) + tags.shape, jnp.int32),
            pltpu.SMEM((nz,) + tags.shape, jnp.int32),
            pltpu.VMEM((ranks, nz, count, side, width), jnp.bfloat16),
            pltpu.VMEM((2 * count, side, inner), jnp.bfloat16),
            pltpu.VMEM((capacity, side, inner), jnp.bfloat16),
            pltpu.VMEM((2 * count * side, capacity * side), jnp.float32),
            result(2 * count, side),
            pltpu.VMEM((2 * side, 2 * full), jnp.bfloat16),
            result(2 * count, side),
            result(2 * ranks, 2 * count, eighth),
            result(2 * ranks, 2 * count, eighth),
            result(nz, 2 * capacity, eighth),
            result(nz, 2 * capacity, eighth),
            result(owned_count, 2 * eighth),
            dma((count,)), dma((count,)), dma((nz, capacity)), dma((nz, capacity)),
            dma((nz,)), dma((nz,)), dma((nz,)), dma((ranks, nz)), dma((ranks, nz)),
            dma((2, ranks)), dma((2, ranks)), dma((nz,)), dma((nz,)), dma((ranks,)), dma((ranks,)),
        ],
        compiler_params=pltpu.CompilerParams(
            vmem_limit_bytes=48 * 1024 * 1024, collective_id=0, has_side_effects=True
        ),
    )(own, occupied, tags, lane, nums)


def shards(integrals, block_list, occupied, owned_blocks):
    block_count, aux_functions, merged = integrals.shape
    aux_count = lax.axis_size("aux")
    norb, nrep = lax.axis_size("orb"), lax.axis_size("rep")
    ranks = norb * nrep
    rank = lax.axis_index("orb") * nrep + lax.axis_index("rep")
    orbital_blocks = owned_blocks.shape[0]
    owned_count = orbital_blocks // aux_count
    side = occupied.shape[0] // orbital_blocks
    depth = aux_functions // ranks
    capacity = max(2, (2 * block_count + aux_count - 1) // aux_count)
    pairs = capacity // 2
    slot_count = aux_count * capacity

    matches = owned_blocks[None, :] == block_list[:, 1:2]
    position = jnp.sum(
        jnp.where(matches, jnp.arange(orbital_blocks, dtype=jnp.int32)[None, :], 0), axis=1
    )
    target = position // owned_count
    numbers = jnp.arange(block_count, dtype=jnp.int32)
    before = (target[None, :] == target[:, None]) & (numbers[None, :] < numbers[:, None])
    slot_of = target * capacity + jnp.sum(before.astype(jnp.int32), axis=1)
    chosen = (
        slot_of[None, :] == jnp.arange(slot_count, dtype=jnp.int32)[:, None]
    ).astype(jnp.int32)

    def by_slot(value, empty):
        return jnp.sum(chosen * (value - empty)[None, :], axis=1) + empty

    local_rows = by_slot(position % owned_count, -1)
    slot_nu = by_slot(block_list[:, 2], 0)[:capacity]
    key = jnp.where(position < SLABB, block_list[:, 0] * SLABB + position, -8)
    slot_key = by_slot(key, -8)[:capacity].reshape(pairs, 2)
    even, odd = slot_key[:, :1], slot_key[:, 1:]
    first = jnp.arange(SLABB * side, dtype=jnp.int32)[None, :] < side
    same = jnp.where(first, even, odd - 1)
    cross = jnp.where(first, odd, even - 1)

    def row(value):
        return jnp.pad(value, (0, SLABB * side - value.shape[0]))[None, :]

    code = jnp.broadcast_to((block_list[:, 0] * SLABB)[:, None], (block_count, SLABB * side))
    slot_pick = by_slot(numbers, 0)
    tags = jnp.concatenate(
        [code, same, cross, row(block_list[:, 2]), row(slot_nu), row(local_rows), row(slot_pick)],
        axis=0,
    )
    tags = jnp.pad(tags, ((0, -tags.shape[0] % 8), (0, 0)))
    nums = jnp.concatenate([row(slot_pick), row(block_list[:, 2]), row(local_rows)], axis=0)
    lanes = jnp.arange(SLABB * side, dtype=jnp.int32)
    inner = lanes % side
    goes = lanes - inner + 2 * (inner % (side // 2)) + inner // (side // 2)
    lane = (goes[:, None] == lanes[None, :]).astype(jnp.float32)

    folds = 32 // depth
    part = lax.dynamic_slice_in_dim(integrals, rank * depth, depth, axis=1)
    part = part.reshape(block_count, 2, depth // 2, folds, merged // folds)
    part = part.transpose(0, 1, 3, 2, 4).reshape(block_count, 2, 16, merged // folds)
    mine = owned_count if owned_count % ranks else owned_count // ranks
    out = exchange(
        (aux_count, norb, nrep), capacity, mine, owned_count,
        part, occupied.reshape(orbital_blocks, side, -1), tags, lane, nums,
    )
    out = out.reshape(mine * side, SLABB * side)
    kept = owned_count * side // ranks
    if mine * side != kept:
        out = lax.dynamic_slice_in_dim(out, rank * kept, kept, axis=0)
    return out


def solution(mesh):
    in_specs = (
        P(("groups", "aux"), None, None),
        P(("groups", "aux"), None),
        P("groups", ("orb", "rep")),
        P("groups"),
    )
    out_specs = P(("groups", "aux", "orb", "rep"), None)
    return jax.shard_map(shards, mesh=mesh, in_specs=in_specs, out_specs=out_specs, check_vma=False)
```

```python
import functools

import jax
import jax.numpy as jnp
from jax import lax
from jax.experimental import pallas as pl
from jax.experimental.pallas import tpu as pltpu
from jax.sharding import PartitionSpec as P

SLABB = 2
MESH = pl.DeviceIdType.MESH


def rows_of(block):
    depth, merged = block.shape
    chunks = merged // 128
    stacked = jnp.stack([block[:, c * 128:(c + 1) * 128] for c in range(chunks)], axis=0)
    return jnp.swapaxes(stacked, 0, 1).reshape(depth * chunks, 128)


def put_piece(block, coeff, diag_ref, out_ref, row):
    ranks = len(coeff)
    side, width = coeff[0].shape
    full = ranks * width
    chunks = block.shape[1] // 128
    folds = side // 2 // chunks
    depth = block.shape[0] // folds
    for r in range(ranks):
        diag_ref[0:side, r * width:(r + 1) * width] = coeff[r]
        diag_ref[side:2 * side, full + r * width:full + (r + 1) * width] = coeff[r]
    piece = jnp.dot(rows_of(block), diag_ref[...], preferred_element_type=jnp.float32)
    for p in range(depth):
        starts = [(h * depth + p) * chunks for h in range(folds)]
        for half in range(2):
            cols = slice(half * full, (half + 1) * full)
            lines = jnp.concatenate([piece[start:start + chunks, cols] for start in starts], axis=0)
            out_ref[
                row, half * (side // 2):(half + 1) * (side // 2), p * full:(p + 1) * full
            ] = lines.astype(jnp.bfloat16)


def kernel(nz, norb, nrep, capacity,
           own_ref, occ_ref, tags_ref, lane_ref, nums_ref, out_ref,
           slots, pairbuf, buf, tagbuf, tagnum, crows, left, right, products, acc, diag,
           natural, chunked, reduced, outgoing, incoming, grouped,
           pair_send, pair_recv, cross_send, cross_recv, tag_send, tag_recv, num_sem,
           row_send, row_recv, a_send, a_recv, b_send, b_recv, c_send, c_recv):
    z = lax.axis_index("aux")
    low = lax.rem(z, 2)
    mate = z + 1 - 2 * low
    rank = lax.axis_index("orb") * nrep + lax.axis_index("rep")
    ranks = norb * nrep
    count = own_ref.shape[0]
    side = lane_ref.shape[0] // SLABB
    pairs = capacity // 2
    eighth = side // (2 * ranks)
    quarter = 2 * eighth
    row_same, row_nu, row_slot = count, count + 2 * pairs, count + 2 * pairs + 1
    row_local, row_pick = count + 2 * pairs + 2, count + 2 * pairs + 3

    def at_z(o):
        return {"aux": lax.rem(z + o, nz)}

    def at_rank(o):
        peer = lax.rem(rank + o, ranks)
        return {"orb": peer // nrep, "rep": lax.rem(peer, nrep)}

    def at_mate(o):
        peer = lax.rem(rank + o, ranks)
        return {"aux": mate, "orb": peer // nrep, "rep": lax.rem(peer, nrep)}

    barrier = pltpu.get_barrier_semaphore()
    for o in range(1, nz):
        pl.semaphore_signal(barrier, inc=1, device_id=at_z(o), device_id_type=MESH)
    for o in range(1, ranks):
        pl.semaphore_signal(barrier, inc=1, device_id=at_rank(o), device_id_type=MESH)
        pl.semaphore_signal(barrier, inc=1, device_id=at_mate(o), device_id_type=MESH)

    for j in range(capacity):
        slots[j] = own_ref[nums_ref[0, j]]
    for k in range(count):
        crows[rank, z, k] = occ_ref[nums_ref[1, k]]
    pl.semaphore_wait(barrier, nz - 1 + 2 * (ranks - 1))

    def remote(src, dst, send, recv, where):
        return pltpu.make_async_remote_copy(
            src_ref=src, dst_ref=dst, send_sem=send, recv_sem=recv,
            device_id=where, device_id_type=MESH,
        )

    def tag_copy(o):
        return remote(tags_ref, tagbuf.at[z], tag_send.at[o], tag_recv.at[o], at_z(o))

    def pair_copy(k):
        return remote(own_ref.at[k, 1 - low], pairbuf.at[k], pair_send.at[k], pair_recv.at[k], {"aux": mate})

    def cross_copy(o, j):
        peer = lax.rem(z + o, nz)
        return remote(
            slots.at[j, lax.rem(peer, 2)], buf.at[z, j], cross_send.at[o, j], cross_recv.at[o, j], at_z(o)
        )

    def row_copy(o, s, size):
        return remote(
            crows.at[rank, s, pl.ds(0, size)], crows.at[rank, s, pl.ds(0, size)],
            row_send.at[o, s], row_recv.at[o, s], at_rank(o),
        )

    for o in range(1, nz):
        tag_copy(o).start()
    for o in range(1, ranks):
        row_copy(o, z, count).start()
    for k in range(count):
        pair_copy(k).start()
    for j in range(capacity):
        for o in range(1, nz):
            peer = lax.rem(z + o, nz)

            @pl.when((peer != mate) & ((peer > z) != (mate > z)))
            def _():
                cross_copy(o, j).start()
    diag[...] = jnp.zeros_like(diag)
    acc[...] = jnp.zeros_like(acc)

    for o in range(1, nz):
        s = lax.rem(z + nz - o, nz)
        tag_copy(o).wait_recv()
        number_copy = pltpu.make_async_copy(tagbuf.at[s], tagnum.at[s], num_sem.at[o])
        number_copy.start()
        number_copy.wait()

        @pl.when(s == mate)
        def _():
            for k in range(count):
                crows[rank, s, k] = occ_ref[tagnum[s, row_nu, k]]
            for p in range(1, ranks):
                row_copy(p, s, count).start()

        @pl.when(s != mate)
        def _():
            for j in range(capacity):
                crows[rank, s, j] = occ_ref[tagnum[s, row_slot, j]]
            for p in range(1, ranks):
                row_copy(p, s, capacity).start()

    def half_transform(block, s, j, out_ref, row):
        coeff = [crows[r, s, j] for r in range(ranks)]
        put_piece(block, coeff, diag, out_ref, row)

    for o in range(1, ranks):
        row_copy(o, z, count).wait_recv()

    def own_body(k, carry):
        half_transform(own_ref[k, low], z, k, left, low * count + k)
        return carry

    lax.fori_loop(0, count, own_body, 0)
    for j in range(capacity):
        for o in range(1, nz):
            peer = lax.rem(z + o, nz)

            @pl.when((peer != mate) & ((peer > z) == (mate > z)))
            def _():
                cross_copy(o, j).start()
    def add_source(same_of, start, sources):
        total = lax.dot_general(
            left[pl.ds(start, len(sources) * count)].reshape(-1, left.shape[2]),
            right[...].reshape(-1, left.shape[2]),
            (((1,), (1,)), ((), ())),
            preferred_element_type=jnp.float32,
        )
        products[0:len(sources) * count * side, :] = total
        for pair in range(pairs):
            for part, source in enumerate(sources):
                tile = products[part * count * side:(part + 1) * count * side, pair * 128:(pair + 1) * 128]
                turned = pltpu.roll(tile, 64, 1).reshape(count, side, 128)
                tile = tile.reshape(count, side, 128)
                code = tagbuf[source, 0:count, :].reshape(count, 1, 128)
                same = same_of(pair)[None] == code
                cross = same_of(pairs + pair)[None] == code
                acc[pl.ds(start + part * count, count)] += (
                    jnp.where(same, tile, 0.0) + jnp.where(cross, turned, 0.0)
                )

    def own_slab(row):
        return tags_ref[row_same + row:row_same + row + 1, :]

    for k in range(count):
        tagbuf[z, k:k + 1, :] = tags_ref[k:k + 1, :]

    for j in range(capacity):
        right[j] = left[nums_ref[0, j] + low * count]
    add_source(own_slab, low * count, [z])
    for o in range(1, ranks):
        row_copy(o, mate, count).wait_recv()

    def mate_body(k, carry):
        pair_copy(k).wait_recv()
        half_transform(pairbuf[k], mate, k, left, (1 - low) * count + k)
        return carry

    lax.fori_loop(0, count, mate_body, 0)
    both = [z - low, z - low + 1]
    add_source(own_slab, (1 - low) * count, [mate])
    for j in range(capacity):
        right[j] = left[tagnum[mate, row_pick, j] + (1 - low) * count]
    add_source(lambda row: tagbuf[mate, row_same + row:row_same + row + 1, :], 0, both)

    def cross_body(step, carry):
        s = z + (1 - 2 * lax.rem(step, 2)) * (step // 2 + 1)
        o = lax.rem(z + nz - s, nz)

        @pl.when((s >= 0) & (s < nz) & (s != mate))
        def _():
            for p in range(1, ranks):
                row_copy(p, s, capacity).wait_recv()

            def slot_body(j, deep):
                cross_copy(o, j).wait_recv()
                half_transform(buf[s, j], s, j, right, j)
                return deep

            lax.fori_loop(0, capacity, slot_body, 0)
            add_source(lambda row: tagbuf[s, row_same + row:row_same + row + 1, :], 0, both)

        return carry

    lax.fori_loop(0, 2 * (nz - 1), cross_body, 0)

    half = side // 2
    flat = jnp.dot(
        acc[...].reshape(2 * count * side, 2 * side), lane_ref[...],
        precision=lax.Precision.HIGHEST, preferred_element_type=jnp.float32,
    )
    for k in range(2 * count):
        for part in range(2):
            start = k * side + part * half
            natural[k, pl.ds(part, half, stride=2), :] = flat[start:start + half]
    for k in range(2 * count):
        for m in range(2 * ranks):
            chunked[m, k] = natural[k, m * eighth:(m + 1) * eighth, :]

    spot = 2 * rank + low

    def a_near(o):
        peer = 2 * lax.rem(rank + o, ranks) + low
        return remote(chunked.at[peer], reduced.at[spot], a_send.at[0, o], a_recv.at[0, o], at_rank(o))

    def a_far(o):
        peer = 2 * lax.rem(rank + o, ranks) + 1 - low
        return remote(chunked.at[peer], reduced.at[spot], a_send.at[1, o], a_recv.at[1, o], at_mate(o))

    for o in range(ranks):
        a_far(o).start()
    for o in range(1, ranks):
        a_near(o).start()
    reduced[spot] = chunked[spot]
    for o in range(1, ranks):
        a_near(o).wait_recv()
    for o in range(ranks):
        a_far(o).wait_recv()
    summed = reduced[0]
    for r in range(1, 2 * ranks):
        summed = summed + reduced[r]

    for slot in range(nz * capacity):
        tagnum[z, row_pick, slot] = nums_ref[0, slot]
        tagnum[z, row_local, slot] = nums_ref[2, slot]
    for t in range(nz):
        for part in range(2):
            for c in range(capacity):
                tag = jnp.full(summed.shape[1:], tagnum[z - low + part, row_pick, t * capacity + c], jnp.int32)
                picked = jnp.zeros(summed.shape[1:], jnp.float32)
                for k in range(count):
                    picked = picked + jnp.where(tag == k, summed[part * count + k], 0.0)
                outgoing[t, part * capacity + c] = picked

    def b_copy(o):
        peer = lax.rem(z + o, nz)
        return remote(outgoing.at[peer], incoming.at[z], b_send.at[o], b_recv.at[o], at_z(o))

    for o in range(1, nz):
        b_copy(o).start()
    incoming[z] = outgoing[z]
    for o in range(1, nz):
        b_copy(o).wait_recv()

    def group_body(row, carry):
        for part in range(2):
            value = jnp.zeros((eighth, 2 * side), jnp.float32)
            for s in range(part, nz, 2):
                for c in range(capacity):
                    for shift, source in ((0, s - part), (capacity, s - part + 1)):
                        tag = jnp.full(value.shape, tagnum[source, row_local, z * capacity + c], jnp.int32)
                        value = value + jnp.where(tag == row, incoming[s, shift + c], 0.0)
            grouped[row, part * eighth:(part + 1) * eighth, :] = value
        return carry

    lax.fori_loop(0, grouped.shape[0], group_body, 0, unroll=5)

    mine = out_ref.shape[0]
    split = mine != grouped.shape[0]

    def c_copy(o):
        peer = lax.rem(rank + o, ranks)
        base = peer * mine if split else 0
        return remote(
            grouped.at[pl.ds(base, mine)],
            out_ref.at[:, pl.ds(pl.multiple_of(rank * quarter, quarter), quarter), :],
            c_send.at[o], c_recv.at[o], at_rank(o),
        )

    for o in range(1, ranks):
        c_copy(o).start()
    base = rank * mine if split else 0
    out_ref[:, pl.ds(pl.multiple_of(rank * quarter, quarter), quarter), :] = grouped[
        pl.ds(base, mine)
    ]
    for o in range(1, ranks):
        c_copy(o).wait_recv()

    for k in range(count):
        pair_copy(k).wait_send()
    for o in range(1, nz):
        tag_copy(o).wait_send()
        b_copy(o).wait_send()

        @pl.when(lax.rem(z + o, nz) != mate)
        def _():
            for j in range(capacity):
                cross_copy(o, j).wait_send()
    for o in range(ranks):
        a_far(o).wait_send()
    for o in range(1, ranks):
        a_near(o).wait_send()
        c_copy(o).wait_send()

    def sent_rows(s, carry):
        @pl.when((s == z) | (s == mate))
        def _():
            for o in range(1, ranks):
                row_copy(o, s, count).wait_send()

        @pl.when((s != z) & (s != mate))
        def _():
            for o in range(1, ranks):
                row_copy(o, s, capacity).wait_send()

        return carry

    lax.fori_loop(0, nz, sent_rows, 0)


def exchange(mesh_shape, capacity, mine, owned_count, own, occupied, tags, lane, nums):
    nz, norb, nrep = mesh_shape
    ranks = norb * nrep
    count, _, lines, merged = own.shape
    width = occupied.shape[2]
    side = lane.shape[0] // SLABB
    full = ranks * width
    inner = lines * merged // (side * side) * full
    eighth = side // (2 * ranks)
    vmem = pl.BlockSpec(memory_space=pltpu.VMEM)
    smem = pl.BlockSpec(memory_space=pltpu.SMEM)
    dma = pltpu.SemaphoreType.DMA

    def result(*lead):
        return pltpu.VMEM(lead + (SLABB * side,), jnp.float32)

    return pl.pallas_call(
        functools.partial(kernel, nz, norb, nrep, capacity),
        out_shape=jax.ShapeDtypeStruct((mine, side, SLABB * side), jnp.float32),
        in_specs=[vmem] * 4 + [smem],
        out_specs=vmem,
        scratch_shapes=[
            pltpu.VMEM((capacity, 2, lines, merged), jnp.bfloat16),
            pltpu.VMEM((count, lines, merged), jnp.bfloat16),
            pltpu.VMEM((nz, capacity, lines, merged), jnp.bfloat16),
            pltpu.VMEM((nz,) + tags.shape, jnp.int32),
            pltpu.SMEM((nz,) + tags.shape, jnp.int32),
            pltpu.VMEM((ranks, nz, count, side, width), jnp.bfloat16),
            pltpu.VMEM((2 * count, side, inner), jnp.bfloat16),
            pltpu.VMEM((capacity, side, inner), jnp.bfloat16),
            pltpu.VMEM((2 * count * side, capacity * side), jnp.float32),
            result(2 * count, side),
            pltpu.VMEM((2 * side, 2 * full), jnp.bfloat16),
            result(2 * count, side),
            result(2 * ranks, 2 * count, eighth),
            result(2 * ranks, 2 * count, eighth),
            result(nz, 2 * capacity, eighth),
            result(nz, 2 * capacity, eighth),
            result(owned_count, 2 * eighth),
            dma((count,)), dma((count,)), dma((nz, capacity)), dma((nz, capacity)),
            dma((nz,)), dma((nz,)), dma((nz,)), dma((ranks, nz)), dma((ranks, nz)),
            dma((2, ranks)), dma((2, ranks)), dma((nz,)), dma((nz,)), dma((ranks,)), dma((ranks,)),
        ],
        compiler_params=pltpu.CompilerParams(
            vmem_limit_bytes=48 * 1024 * 1024, collective_id=0, has_side_effects=True
        ),
    )(own, occupied, tags, lane, nums)


def shards(integrals, block_list, occupied, owned_blocks):
    block_count, aux_functions, merged = integrals.shape
    aux_count = lax.axis_size("aux")
    norb, nrep = lax.axis_size("orb"), lax.axis_size("rep")
    ranks = norb * nrep
    rank = lax.axis_index("orb") * nrep + lax.axis_index("rep")
    orbital_blocks = owned_blocks.shape[0]
    owned_count = orbital_blocks // aux_count
    side = occupied.shape[0] // orbital_blocks
    depth = aux_functions // ranks
    capacity = max(2, (2 * block_count + aux_count - 1) // aux_count)
    pairs = capacity // 2
    slot_count = aux_count * capacity

    matches = owned_blocks[None, :] == block_list[:, 1:2]
    position = jnp.sum(
        jnp.where(matches, jnp.arange(orbital_blocks, dtype=jnp.int32)[None, :], 0), axis=1
    )
    target = position // owned_count
    numbers = jnp.arange(block_count, dtype=jnp.int32)
    before = (target[None, :] == target[:, None]) & (numbers[None, :] < numbers[:, None])
    slot_of = target * capacity + jnp.sum(before.astype(jnp.int32), axis=1)
    chosen = (
        slot_of[None, :] == jnp.arange(slot_count, dtype=jnp.int32)[:, None]
    ).astype(jnp.int32)

    def by_slot(value, empty):
        return jnp.sum(chosen * (value - empty)[None, :], axis=1) + empty

    local_rows = by_slot(position % owned_count, -1)
    slot_nu = by_slot(block_list[:, 2], 0)[:capacity]
    key = jnp.where(position < SLABB, block_list[:, 0] * SLABB + position, -8)
    slot_key = by_slot(key, -8)[:capacity].reshape(pairs, 2)
    even, odd = slot_key[:, :1], slot_key[:, 1:]
    first = jnp.arange(SLABB * side, dtype=jnp.int32)[None, :] < side
    same = jnp.where(first, even, odd - 1)
    cross = jnp.where(first, odd, even - 1)

    def row(value):
        return jnp.pad(value, (0, SLABB * side - value.shape[0]))[None, :]

    code = jnp.broadcast_to((block_list[:, 0] * SLABB)[:, None], (block_count, SLABB * side))
    slot_pick = by_slot(numbers, 0)
    tags = jnp.concatenate(
        [code, same, cross, row(block_list[:, 2]), row(slot_nu), row(local_rows), row(slot_pick)],
        axis=0,
    )
    tags = jnp.pad(tags, ((0, -tags.shape[0] % 8), (0, 0)))
    nums = jnp.concatenate([row(slot_pick), row(block_list[:, 2]), row(local_rows)], axis=0)
    lanes = jnp.arange(SLABB * side, dtype=jnp.int32)
    inner = lanes % side
    goes = lanes - inner + 2 * (inner % (side // 2)) + inner // (side // 2)
    lane = (goes[:, None] == lanes[None, :]).astype(jnp.float32)

    folds = 32 // depth
    part = lax.dynamic_slice_in_dim(integrals, rank * depth, depth, axis=1)
    part = part.reshape(block_count, 2, depth // 2, folds, merged // folds)
    part = part.transpose(0, 1, 3, 2, 4).reshape(block_count, 2, 16, merged // folds)
    mine = owned_count if owned_count % ranks else owned_count // ranks
    out = exchange(
        (aux_count, norb, nrep), capacity, mine, owned_count,
        part, occupied.reshape(orbital_blocks, side, -1), tags, lane, nums,
    )
    out = out.reshape(mine * side, SLABB * side)
    kept = owned_count * side // ranks
    if mine * side != kept:
        out = lax.dynamic_slice_in_dim(out, rank * kept, kept, axis=0)
    return out


def solution(mesh):
    in_specs = (
        P(("groups", "aux"), None, None),
        P(("groups", "aux"), None),
        P("groups", ("orb", "rep")),
        P("groups"),
    )
    out_specs = P(("groups", "aux", "orb", "rep"), None)
    return jax.shard_map(shards, mesh=mesh, in_specs=in_specs, out_specs=out_specs, check_vma=False)
```

```python
import functools

import jax
import jax.numpy as jnp
from jax import lax
from jax.experimental import pallas as pl
from jax.experimental.pallas import tpu as pltpu
from jax.sharding import PartitionSpec as P

SLABB = 2
MESH = pl.DeviceIdType.MESH


def rows_of(block):
    depth, merged = block.shape
    chunks = merged // 128
    stacked = jnp.stack([block[:, c * 128:(c + 1) * 128] for c in range(chunks)], axis=0)
    return jnp.swapaxes(stacked, 0, 1).reshape(depth * chunks, 128)


def put_piece(block, coeff, diag_ref, out_ref, row):
    ranks = len(coeff)
    side, width = coeff[0].shape
    full = ranks * width
    chunks = block.shape[1] // 128
    folds = side // 2 // chunks
    depth = block.shape[0] // folds
    for r in range(ranks):
        diag_ref[0:side, r * width:(r + 1) * width] = coeff[r]
        diag_ref[side:2 * side, full + r * width:full + (r + 1) * width] = coeff[r]
    piece = jnp.dot(rows_of(block), diag_ref[...], preferred_element_type=jnp.float32)
    for p in range(depth):
        starts = [(h * depth + p) * chunks for h in range(folds)]
        for half in range(2):
            cols = slice(half * full, (half + 1) * full)
            lines = jnp.concatenate([piece[start:start + chunks, cols] for start in starts], axis=0)
            out_ref[
                row, half * (side // 2):(half + 1) * (side // 2), p * full:(p + 1) * full
            ] = lines.astype(jnp.bfloat16)


def kernel(nz, norb, nrep, capacity,
           own_ref, occ_ref, tags_ref, lane_ref, nums_ref, out_ref,
           slots, pairbuf, buf, tagbuf, tagnum, crows, left, right, products, acc, diag,
           natural, chunked, reduced, outgoing, incoming, grouped,
           pair_send, pair_recv, cross_send, cross_recv, tag_send, tag_recv, num_sem,
           row_send, row_recv, a_send, a_recv, b_send, b_recv, c_send, c_recv):
    z = lax.axis_index("aux")
    low = lax.rem(z, 2)
    mate = z + 1 - 2 * low
    rank = lax.axis_index("orb") * nrep + lax.axis_index("rep")
    ranks = norb * nrep
    count = own_ref.shape[0]
    side = lane_ref.shape[0] // SLABB
    pairs = capacity // 2
    eighth = side // (2 * ranks)
    quarter = 2 * eighth
    row_same, row_nu, row_slot = count, count + 2 * pairs, count + 2 * pairs + 1
    row_local, row_pick = count + 2 * pairs + 2, count + 2 * pairs + 3

    def at_z(o):
        return {"aux": lax.rem(z + o, nz)}

    def at_rank(o):
        peer = lax.rem(rank + o, ranks)
        return {"orb": peer // nrep, "rep": lax.rem(peer, nrep)}

    def at_mate(o):
        peer = lax.rem(rank + o, ranks)
        return {"aux": mate, "orb": peer // nrep, "rep": lax.rem(peer, nrep)}

    barrier = pltpu.get_barrier_semaphore()
    for o in range(1, nz):
        pl.semaphore_signal(barrier, inc=1, device_id=at_z(o), device_id_type=MESH)
    for o in range(1, ranks):
        pl.semaphore_signal(barrier, inc=1, device_id=at_rank(o), device_id_type=MESH)
        pl.semaphore_signal(barrier, inc=1, device_id=at_mate(o), device_id_type=MESH)

    for j in range(capacity):
        slots[j] = own_ref[nums_ref[0, j]]
    for k in range(count):
        crows[rank, z, k] = occ_ref[nums_ref[1, k]]
    pl.semaphore_wait(barrier, nz - 1 + 2 * (ranks - 1))

    def remote(src, dst, send, recv, where):
        return pltpu.make_async_remote_copy(
            src_ref=src, dst_ref=dst, send_sem=send, recv_sem=recv,
            device_id=where, device_id_type=MESH,
        )

    def tag_copy(o):
        return remote(tags_ref, tagbuf.at[z], tag_send.at[o], tag_recv.at[o], at_z(o))

    def pair_copy(k):
        return remote(own_ref.at[k, 1 - low], pairbuf.at[k], pair_send.at[k], pair_recv.at[k], {"aux": mate})

    def cross_copy(o, j):
        peer = lax.rem(z + o, nz)
        return remote(
            slots.at[j, lax.rem(peer, 2)], buf.at[z, j], cross_send.at[o, j], cross_recv.at[o, j], at_z(o)
        )

    def row_copy(o, s, size):
        return remote(
            crows.at[rank, s, pl.ds(0, size)], crows.at[rank, s, pl.ds(0, size)],
            row_send.at[o, s], row_recv.at[o, s], at_rank(o),
        )

    for o in range(1, nz):
        tag_copy(o).start()
    for o in range(1, ranks):
        row_copy(o, z, count).start()
    for k in range(count):
        pair_copy(k).start()
    for j in range(capacity):
        for o in range(1, nz):
            peer = lax.rem(z + o, nz)

            @pl.when((peer != mate) & ((peer > z) != (mate > z)))
            def _():
                cross_copy(o, j).start()
    diag[...] = jnp.zeros_like(diag)
    acc[...] = jnp.zeros_like(acc)

    for o in range(1, nz):
        s = lax.rem(z + nz - o, nz)
        tag_copy(o).wait_recv()
        number_copy = pltpu.make_async_copy(tagbuf.at[s], tagnum.at[s], num_sem.at[o])
        number_copy.start()
        number_copy.wait()

        @pl.when(s == mate)
        def _():
            for k in range(count):
                crows[rank, s, k] = occ_ref[tagnum[s, row_nu, k]]
            for p in range(1, ranks):
                row_copy(p, s, count).start()

        @pl.when(s != mate)
        def _():
            for j in range(capacity):
                crows[rank, s, j] = occ_ref[tagnum[s, row_slot, j]]
            for p in range(1, ranks):
                row_copy(p, s, capacity).start()

    def half_transform(block, s, j, out_ref, row):
        coeff = [crows[r, s, j] for r in range(ranks)]
        put_piece(block, coeff, diag, out_ref, row)

    for o in range(1, ranks):
        row_copy(o, z, count).wait_recv()

    def own_body(k, carry):
        half_transform(own_ref[k, low], z, k, left, low * count + k)
        return carry

    lax.fori_loop(0, count, own_body, 0)
    for j in range(capacity):
        for o in range(1, nz):
            peer = lax.rem(z + o, nz)

            @pl.when((peer != mate) & ((peer > z) == (mate > z)))
            def _():
                cross_copy(o, j).start()
    def add_source(same_of, start, sources):
        total = lax.dot_general(
            left[pl.ds(start, len(sources) * count)].reshape(-1, left.shape[2]),
            right[...].reshape(-1, left.shape[2]),
            (((1,), (1,)), ((), ())),
            preferred_element_type=jnp.float32,
        )
        products[0:len(sources) * count * side, :] = total
        for pair in range(pairs):
            for part, source in enumerate(sources):
                tile = products[part * count * side:(part + 1) * count * side, pair * 128:(pair + 1) * 128]
                turned = pltpu.roll(tile, 64, 1).reshape(count, side, 128)
                tile = tile.reshape(count, side, 128)
                code = tagbuf[source, 0:count, :].reshape(count, 1, 128)
                same = same_of(pair)[None] == code
                cross = same_of(pairs + pair)[None] == code
                acc[pl.ds(start + part * count, count)] += (
                    jnp.where(same, tile, 0.0) + jnp.where(cross, turned, 0.0)
                )

    def own_slab(row):
        return tags_ref[row_same + row:row_same + row + 1, :]

    for k in range(count):
        tagbuf[z, k:k + 1, :] = tags_ref[k:k + 1, :]

    for j in range(capacity):
        right[j] = left[nums_ref[0, j] + low * count]
    add_source(own_slab, low * count, [z])
    for o in range(1, ranks):
        row_copy(o, mate, count).wait_recv()

    def mate_body(k, carry):
        pair_copy(k).wait_recv()
        half_transform(pairbuf[k], mate, k, left, (1 - low) * count + k)
        return carry

    lax.fori_loop(0, count, mate_body, 0)
    both = [z - low, z - low + 1]
    add_source(own_slab, (1 - low) * count, [mate])
    for j in range(capacity):
        right[j] = left[tagnum[mate, row_pick, j] + (1 - low) * count]
    add_source(lambda row: tagbuf[mate, row_same + row:row_same + row + 1, :], 0, both)

    def cross_body(step, carry):
        s = z + (1 - 2 * lax.rem(step, 2)) * (step // 2 + 1)
        o = lax.rem(z + nz - s, nz)

        @pl.when((s >= 0) & (s < nz) & (s != mate))
        def _():
            for p in range(1, ranks):
                row_copy(p, s, capacity).wait_recv()

            def slot_body(j, deep):
                cross_copy(o, j).wait_recv()
                half_transform(buf[s, j], s, j, right, j)
                return deep

            lax.fori_loop(0, capacity, slot_body, 0)
            add_source(lambda row: tagbuf[s, row_same + row:row_same + row + 1, :], 0, both)

        return carry

    lax.fori_loop(0, 2 * (nz - 1), cross_body, 0)

    spot = 2 * rank + low

    def a_near(o, part):
        peer = 2 * lax.rem(rank + o, ranks) + low
        blocks = pl.ds(part * count, count)
        return remote(
            chunked.at[peer, blocks], reduced.at[spot, blocks],
            a_send.at[0, part, o], a_recv.at[0, part, o], at_rank(o),
        )

    def a_far(o, part):
        peer = 2 * lax.rem(rank + o, ranks) + 1 - low
        blocks = pl.ds(part * count, count)
        return remote(
            chunked.at[peer, blocks], reduced.at[spot, blocks],
            a_send.at[1, part, o], a_recv.at[1, part, o], at_mate(o),
        )

    half = side // 2
    for part in range(2):
        flat = jnp.dot(
            acc[part * count:(part + 1) * count].reshape(count * side, 2 * side), lane_ref[...],
            precision=lax.Precision.HIGHEST, preferred_element_type=jnp.float32,
        )
        for k in range(count):
            block = part * count + k
            for odd in range(2):
                start = k * side + odd * half
                natural[block, pl.ds(odd, half, stride=2), :] = flat[start:start + half]
        for block in range(part * count, (part + 1) * count):
            for m in range(2 * ranks):
                chunked[m, block] = natural[block, m * eighth:(m + 1) * eighth, :]
        for o in range(ranks):
            a_far(o, part).start()
        for o in range(1, ranks):
            a_near(o, part).start()
    reduced[spot] = chunked[spot]
    for part in range(2):
        for o in range(1, ranks):
            a_near(o, part).wait_recv()
        for o in range(ranks):
            a_far(o, part).wait_recv()
    summed = reduced[0]
    for r in range(1, 2 * ranks):
        summed = summed + reduced[r]

    for slot in range(nz * capacity):
        tagnum[z, row_pick, slot] = nums_ref[0, slot]
        tagnum[z, row_local, slot] = nums_ref[2, slot]
    for t in range(nz):
        for part in range(2):
            for c in range(capacity):
                tag = jnp.full(summed.shape[1:], tagnum[z - low + part, row_pick, t * capacity + c], jnp.int32)
                picked = jnp.zeros(summed.shape[1:], jnp.float32)
                for k in range(count):
                    picked = picked + jnp.where(tag == k, summed[part * count + k], 0.0)
                outgoing[t, part * capacity + c] = picked

    def b_copy(o):
        peer = lax.rem(z + o, nz)
        return remote(outgoing.at[peer], incoming.at[z], b_send.at[o], b_recv.at[o], at_z(o))

    for o in range(1, nz):
        b_copy(o).start()
    incoming[z] = outgoing[z]
    for o in range(1, nz):
        b_copy(o).wait_recv()

    def group_body(row, carry):
        for part in range(2):
            value = jnp.zeros((eighth, 2 * side), jnp.float32)
            for s in range(part, nz, 2):
                for c in range(capacity):
                    for shift, source in ((0, s - part), (capacity, s - part + 1)):
                        tag = jnp.full(value.shape, tagnum[source, row_local, z * capacity + c], jnp.int32)
                        value = value + jnp.where(tag == row, incoming[s, shift + c], 0.0)
            grouped[row, part * eighth:(part + 1) * eighth, :] = value
        return carry

    lax.fori_loop(0, grouped.shape[0], group_body, 0, unroll=5)

    mine = out_ref.shape[0]
    split = mine != grouped.shape[0]

    def c_copy(o):
        peer = lax.rem(rank + o, ranks)
        base = peer * mine if split else 0
        return remote(
            grouped.at[pl.ds(base, mine)],
            out_ref.at[:, pl.ds(pl.multiple_of(rank * quarter, quarter), quarter), :],
            c_send.at[o], c_recv.at[o], at_rank(o),
        )

    for o in range(1, ranks):
        c_copy(o).start()
    base = rank * mine if split else 0
    out_ref[:, pl.ds(pl.multiple_of(rank * quarter, quarter), quarter), :] = grouped[
        pl.ds(base, mine)
    ]
    for o in range(1, ranks):
        c_copy(o).wait_recv()

    for k in range(count):
        pair_copy(k).wait_send()
    for o in range(1, nz):
        tag_copy(o).wait_send()
        b_copy(o).wait_send()

        @pl.when(lax.rem(z + o, nz) != mate)
        def _():
            for j in range(capacity):
                cross_copy(o, j).wait_send()
    for o in range(ranks):
        a_far(o, 0).wait_send()
        a_far(o, 1).wait_send()
    for o in range(1, ranks):
        a_near(o, 0).wait_send()
        a_near(o, 1).wait_send()
        c_copy(o).wait_send()

    def sent_rows(s, carry):
        @pl.when((s == z) | (s == mate))
        def _():
            for o in range(1, ranks):
                row_copy(o, s, count).wait_send()

        @pl.when((s != z) & (s != mate))
        def _():
            for o in range(1, ranks):
                row_copy(o, s, capacity).wait_send()

        return carry

    lax.fori_loop(0, nz, sent_rows, 0)


def exchange(mesh_shape, capacity, mine, owned_count, own, occupied, tags, lane, nums):
    nz, norb, nrep = mesh_shape
    ranks = norb * nrep
    count, _, lines, merged = own.shape
    width = occupied.shape[2]
    side = lane.shape[0] // SLABB
    full = ranks * width
    inner = lines * merged // (side * side) * full
    eighth = side // (2 * ranks)
    vmem = pl.BlockSpec(memory_space=pltpu.VMEM)
    smem = pl.BlockSpec(memory_space=pltpu.SMEM)
    dma = pltpu.SemaphoreType.DMA

    def result(*lead):
        return pltpu.VMEM(lead + (SLABB * side,), jnp.float32)

    return pl.pallas_call(
        functools.partial(kernel, nz, norb, nrep, capacity),
        out_shape=jax.ShapeDtypeStruct((mine, side, SLABB * side), jnp.float32),
        in_specs=[vmem] * 4 + [smem],
        out_specs=vmem,
        scratch_shapes=[
            pltpu.VMEM((capacity, 2, lines, merged), jnp.bfloat16),
            pltpu.VMEM((count, lines, merged), jnp.bfloat16),
            pltpu.VMEM((nz, capacity, lines, merged), jnp.bfloat16),
            pltpu.VMEM((nz,) + tags.shape, jnp.int32),
            pltpu.SMEM((nz,) + tags.shape, jnp.int32),
            pltpu.VMEM((ranks, nz, count, side, width), jnp.bfloat16),
            pltpu.VMEM((2 * count, side, inner), jnp.bfloat16),
            pltpu.VMEM((capacity, side, inner), jnp.bfloat16),
            pltpu.VMEM((2 * count * side, capacity * side), jnp.float32),
            result(2 * count, side),
            pltpu.VMEM((2 * side, 2 * full), jnp.bfloat16),
            result(2 * count, side),
            result(2 * ranks, 2 * count, eighth),
            result(2 * ranks, 2 * count, eighth),
            result(nz, 2 * capacity, eighth),
            result(nz, 2 * capacity, eighth),
            result(owned_count, 2 * eighth),
            dma((count,)), dma((count,)), dma((nz, capacity)), dma((nz, capacity)),
            dma((nz,)), dma((nz,)), dma((nz,)), dma((ranks, nz)), dma((ranks, nz)),
            dma((2, 2, ranks)), dma((2, 2, ranks)), dma((nz,)), dma((nz,)), dma((ranks,)), dma((ranks,)),
        ],
        compiler_params=pltpu.CompilerParams(
            vmem_limit_bytes=48 * 1024 * 1024, collective_id=0, has_side_effects=True
        ),
    )(own, occupied, tags, lane, nums)


def shards(integrals, block_list, occupied, owned_blocks):
    block_count, aux_functions, merged = integrals.shape
    aux_count = lax.axis_size("aux")
    norb, nrep = lax.axis_size("orb"), lax.axis_size("rep")
    ranks = norb * nrep
    rank = lax.axis_index("orb") * nrep + lax.axis_index("rep")
    orbital_blocks = owned_blocks.shape[0]
    owned_count = orbital_blocks // aux_count
    side = occupied.shape[0] // orbital_blocks
    depth = aux_functions // ranks
    capacity = max(2, (2 * block_count + aux_count - 1) // aux_count)
    pairs = capacity // 2
    slot_count = aux_count * capacity

    matches = owned_blocks[None, :] == block_list[:, 1:2]
    position = jnp.sum(
        jnp.where(matches, jnp.arange(orbital_blocks, dtype=jnp.int32)[None, :], 0), axis=1
    )
    target = position // owned_count
    numbers = jnp.arange(block_count, dtype=jnp.int32)
    before = (target[None, :] == target[:, None]) & (numbers[None, :] < numbers[:, None])
    slot_of = target * capacity + jnp.sum(before.astype(jnp.int32), axis=1)
    chosen = (
        slot_of[None, :] == jnp.arange(slot_count, dtype=jnp.int32)[:, None]
    ).astype(jnp.int32)

    def by_slot(value, empty):
        return jnp.sum(chosen * (value - empty)[None, :], axis=1) + empty

    local_rows = by_slot(position % owned_count, -1)
    slot_nu = by_slot(block_list[:, 2], 0)[:capacity]
    key = jnp.where(position < SLABB, block_list[:, 0] * SLABB + position, -8)
    slot_key = by_slot(key, -8)[:capacity].reshape(pairs, 2)
    even, odd = slot_key[:, :1], slot_key[:, 1:]
    first = jnp.arange(SLABB * side, dtype=jnp.int32)[None, :] < side
    same = jnp.where(first, even, odd - 1)
    cross = jnp.where(first, odd, even - 1)

    def row(value):
        return jnp.pad(value, (0, SLABB * side - value.shape[0]))[None, :]

    code = jnp.broadcast_to((block_list[:, 0] * SLABB)[:, None], (block_count, SLABB * side))
    slot_pick = by_slot(numbers, 0)
    tags = jnp.concatenate(
        [code, same, cross, row(block_list[:, 2]), row(slot_nu), row(local_rows), row(slot_pick)],
        axis=0,
    )
    tags = jnp.pad(tags, ((0, -tags.shape[0] % 8), (0, 0)))
    nums = jnp.concatenate([row(slot_pick), row(block_list[:, 2]), row(local_rows)], axis=0)
    lanes = jnp.arange(SLABB * side, dtype=jnp.int32)
    inner = lanes % side
    goes = lanes - inner + 2 * (inner % (side // 2)) + inner // (side // 2)
    lane = (goes[:, None] == lanes[None, :]).astype(jnp.float32)

    folds = 32 // depth
    part = lax.dynamic_slice_in_dim(integrals, rank * depth, depth, axis=1)
    part = part.reshape(block_count, 2, depth // 2, folds, merged // folds)
    part = part.transpose(0, 1, 3, 2, 4).reshape(block_count, 2, 16, merged // folds)
    mine = owned_count if owned_count % ranks else owned_count // ranks
    out = exchange(
        (aux_count, norb, nrep), capacity, mine, owned_count,
        part, occupied.reshape(orbital_blocks, side, -1), tags, lane, nums,
    )
    out = out.reshape(mine * side, SLABB * side)
    kept = owned_count * side // ranks
    if mine * side != kept:
        out = lax.dynamic_slice_in_dim(out, rank * kept, kept, axis=0)
    return out


def solution(mesh):
    in_specs = (
        P(("groups", "aux"), None, None),
        P(("groups", "aux"), None),
        P("groups", ("orb", "rep")),
        P("groups"),
    )
    out_specs = P(("groups", "aux", "orb", "rep"), None)
    return jax.shard_map(shards, mesh=mesh, in_specs=in_specs, out_specs=out_specs, check_vma=False)
```
